128 devices in a mesh: dom: 32 (over x, z, core), grp: 4 (over y).
Axes of the slice: x: 4, y: 4, z: 4, core: 2. Of those that a mesh axis runs over, the one named last changes fastest.
Arguments:
- embed: float32 [32768, 256], P('dom'), may hold values from -6 to 6
- cotangent: float32 [32768, 256], P('dom'), may hold values from -6 to 6
- first_moment: float32 [32768, 256], P('dom'), may hold values from -4 to 4
- second_moment: float32 [32768, 256], P('dom'), may hold values from 0.1 to 4
- degrees: int32 [32768], P('dom'), may hold values from 16 to 128
- tiles: float32 [32, 4, 128, 128, 128], P('dom', 'grp'), may hold values from 0.05 to 1
- tile_rows: int32 [32, 4, 128], P('dom', 'grp'), may hold values from 0 to 7, as said below
- tile_cols: int32 [32, 4, 128], P('dom', 'grp'), may hold values from 0 to 39
- tile_count: int32 [32, 4], P('dom', 'grp'), may hold values from 16 to 128, as said below
- send_list: int32 [32, 32, 1], P('dom'), may hold values from 0 to 7
Outputs:
- final: float32 [32768, 256], P('dom')
- new_embed: float32 [32768, 256], P('dom')
- new_first: float32 [32768, 256], P('dom')
- new_second: float32 [32768, 256], P('dom')
The draws below stay inside these ranges and needn't reach their ends.
Inputs may be any that keep to these rules, and one draw needn't show every extreme that they name: `tile_rows`: a row block of the partition; in every partition one hub block holds about half of all tile slots, spread over all helpers. `tile_count`: in every partition one helper has all 128 slots live, the others between 16 and 64.
All inputs are finite; a program needn't handle non-finite values.
Results may differ from the reference program's by a relative error of at most 0.0003.
Values sent between devices are 32-bit elements; how exact they have to be, the bound alone decides.
No kernel may reach another device: no remote copies, remote signals or barrier semaphores. Data moves between devices by JAX's collectives and lax.ppermute only.
A program may use at most 192 MiB of HBM per device.

```python
import math
import jax
import jax.numpy as jnp
from jax import lax

F = 256
BLK = 128
PB = 8
TILES_DEV = 128
SLOTS = 1
LAYERS = 2
STEP = 10
PARTITIONS = 32
HELPERS = 4
COLS = 40
NODES = 32768


def draw_tile_rows(key, part):
    key = jax.random.fold_in(key, 2)
    key_hub, key_spread, key_pick = jax.random.split(key, 3)
    hub = jax.random.randint(key_hub, (PARTITIONS, 1, 1), 0, PB)
    spread = jax.random.randint(key_spread, (PARTITIONS, HELPERS, TILES_DEV), 0, PB)
    pick = jax.random.randint(key_pick, (PARTITIONS, HELPERS, TILES_DEV), 0, 2)
    return jnp.where(pick == 0, hub, spread).astype(jnp.int32)


def draw_tile_count(key, part):
    key = jax.random.fold_in(key, 5)
    key_base, key_full = jax.random.split(key, 2)
    base = jax.random.randint(key_base, (PARTITIONS, HELPERS), TILES_DEV // 8, TILES_DEV // 2 + 1)
    full = jax.random.randint(key_full, (PARTITIONS,), 0, HELPERS)
    chosen = jnp.arange(HELPERS)[None, :] == full[:, None]
    return jnp.where(chosen, TILES_DEV, base).astype(jnp.int32)


def plant(result, stream_key, low, high):
    extent = result.shape
    place = [jax.random.randint(jax.random.fold_in(stream_key, axis), (), 0, extent[axis]) for axis in range(len(extent))]
    result = result.at[tuple(place)].set(low)
    longest = extent.index(max(extent))
    place[longest] = (place[longest] + 1) % extent[longest]
    return result.at[tuple(place)].set(high)


def steps_of(key, dims, cuts, low, high):
    factor_of = 1.0
    for position, parts in cuts:
        heights = jax.random.uniform(jax.random.fold_in(jax.random.fold_in(key, 6), position), (parts,), jnp.float32, low / len(cuts), high / len(cuts))
        factor_of = factor_of * jnp.repeat(jnp.exp(heights), dims[position] // parts).reshape((-1,) + (1,) * (len(dims) - 1 - position))
    return factor_of


def centred(stream_key, dims, scale, reach, shards=(), held_as=jnp.bfloat16):
    array = scale * jax.random.normal(stream_key, dims, jnp.float32)
    if shards:
        array = array * steps_of(stream_key, dims, shards, -0.22, 0.18)
    return jnp.clip(array, -reach, reach).astype(held_as)


def setup_inputs(seed: int = 0) -> dict:
    arg_keys = jax.random.split(jax.random.key(seed), 11)
    return {
        "embed": centred(arg_keys[0], (NODES, F), 1.0, 6.0, ((0, 32),), jnp.float32),
        "cotangent": centred(arg_keys[1], (NODES, F), 1.0, 6.0, ((0, 32),), jnp.float32),
        "first_moment": centred(arg_keys[2], (NODES, F), 0.5, 4.0, ((0, 32),), jnp.float32),
        "second_moment": jnp.clip(jnp.exp(math.log(4.0) - 3.6888794 * jax.random.uniform(arg_keys[3], (NODES, F), jnp.float32) ** steps_of(arg_keys[3], (NODES, F), ((0, 32),), -0.2, 0.2)), 0.1, 4.0),
        "degrees": plant(jax.random.randint(arg_keys[4], (NODES,), max(2, BLK // 8), BLK + 1), jax.random.fold_in(arg_keys[4], 1), max(2, BLK // 8), BLK).astype(jnp.int32),
        "tiles": jnp.clip(0.05 + 0.95 * jax.random.uniform(arg_keys[5], (PARTITIONS, HELPERS, TILES_DEV, BLK, BLK), jnp.float32) ** steps_of(arg_keys[5], (PARTITIONS, HELPERS, TILES_DEV, BLK, BLK), ((0, 32), (1, 4)), -0.2, 0.2), 0.05, 1.0),
        "tile_rows": draw_tile_rows(jax.random.fold_in(arg_keys[10], 71), 0),
        "tile_cols": plant(jax.random.randint(arg_keys[7], (PARTITIONS, HELPERS, TILES_DEV), 0, COLS), jax.random.fold_in(arg_keys[7], 1), 0, COLS - 1).astype(jnp.int32),
        "tile_count": draw_tile_count(jax.random.fold_in(arg_keys[10], 71), 0),
        "send_list": plant(jax.random.randint(arg_keys[9], (PARTITIONS, PARTITIONS, SLOTS), 0, PB), jax.random.fold_in(arg_keys[9], 1), 0, PB - 1).astype(jnp.int32),
    }


def live_mask(counts):
    return (jnp.arange(TILES_DEV)[None, :] < counts[:, None]).reshape(-1).astype(jnp.float32)

def forward_pass(scaled, tiles, tile_rows, tile_cols, tile_count, send_list):
    senders = jnp.arange(PARTITIONS)

    def one_part(part_index):
        arrived = scaled[senders[:, None], send_list[:, part_index, :]]
        space = jnp.concatenate([scaled[part_index], arrived.reshape(PARTITIONS * SLOTS, BLK, F)], 0)
        mats = tiles[part_index].reshape(HELPERS * TILES_DEV, BLK, BLK)
        rows = tile_rows[part_index].reshape(-1)
        cols = tile_cols[part_index].reshape(-1)
        live = live_mask(tile_count[part_index])
        prod = jnp.einsum('tij,tjf->tif', mats, space[cols], precision=lax.Precision.HIGHEST) * live[:, None, None]
        table = (rows[:, None] == jnp.arange(PB)[None, :]).astype(jnp.float32)
        return jnp.einsum('tb,tif->bif', table, prod, precision=lax.Precision.HIGHEST)
    return lax.map(one_part, jnp.arange(PARTITIONS))

def backward_pass(scaled, tiles, tile_rows, tile_cols, tile_count, send_list):

    def one_part(part_index):
        mats = tiles[part_index].reshape(HELPERS * TILES_DEV, BLK, BLK)
        rows = tile_rows[part_index].reshape(-1)
        cols = tile_cols[part_index].reshape(-1)
        live = live_mask(tile_count[part_index])
        picked = scaled[part_index][rows]
        prod = jnp.einsum('tji,tjf->tif', mats, picked, precision=lax.Precision.HIGHEST) * live[:, None, None]
        table = (cols[:, None] == jnp.arange(COLS)[None, :]).astype(jnp.float32)
        return jnp.einsum('tc,tif->cif', table, prod, precision=lax.Precision.HIGHEST)
    contrib = lax.map(one_part, jnp.arange(PARTITIONS))
    local_part = contrib[:, :PB]
    remote = contrib[:, PB:].reshape(PARTITIONS, PARTITIONS, SLOTS, BLK, F)
    owners = (send_list[:, :, :, None] == jnp.arange(PB)[None, None, None, :]).astype(jnp.float32)
    returned = jnp.einsum('qpsb,pqsif->qbif', owners, remote, precision=lax.Precision.HIGHEST)
    return local_part + returned

def reference(embed, cotangent, first_moment, second_moment, degrees, tiles, tile_rows, tile_cols, tile_count, send_list):
    scale = (1.0 / jnp.sqrt(degrees.astype(jnp.float32))).reshape(PARTITIONS, PB, BLK, 1)
    current = embed.reshape(PARTITIONS, PB, BLK, F)
    total = current
    for layer_index in range(LAYERS):
        current = scale * forward_pass(scale * current, tiles, tile_rows, tile_cols, tile_count, send_list)
        total = total + current
    final = (total / (LAYERS + 1)).reshape(NODES, F)
    share = cotangent.reshape(PARTITIONS, PB, BLK, F) / (LAYERS + 1)
    grad = share
    for layer_index in range(LAYERS):
        grad = share + scale * backward_pass(scale * grad, tiles, tile_rows, tile_cols, tile_count, send_list)
    grad = grad.reshape(NODES, F)
    new_first = 0.9 * first_moment + 0.1 * grad
    new_second = 0.999 * second_moment + 0.001 * grad * grad
    corrected_first = new_first / (1.0 - 0.9 ** STEP)
    corrected_second = new_second / (1.0 - 0.999 ** STEP)
    new_embed = embed - 0.01 * corrected_first / (jnp.sqrt(corrected_second) + 1e-08)
    return (final, new_embed, new_first, new_second)
```

```python
import functools

import jax
import jax.numpy as jnp
from jax import lax
from jax.experimental import pallas as pl
from jax.experimental.pallas import tpu as pltpu
from jax.sharding import PartitionSpec as P

LAYERS = 2
STEP = 10
CHUNKS = 8
UNROLL = 8
MIB = 2**20

SMEM = pl.BlockSpec(memory_space=pltpu.SMEM)
VMEM = pl.BlockSpec(memory_space=pltpu.VMEM)
ANY = pl.BlockSpec(memory_space=pl.ANY)


def f32(*shape):
    return jax.ShapeDtypeStruct(shape, jnp.float32)


def params(mib):
    return pltpu.CompilerParams(vmem_limit_bytes=mib * MIB)


def cost(us):
    return pl.CostEstimate(flops=0, bytes_accessed=int(us * 3.6e6), transcendentals=0)


def split(x):
    hi = x.astype(jnp.bfloat16)
    lo = (x - hi.astype(jnp.float32)).astype(jnp.bfloat16)
    return hi, lo


def store_split(xs, c, x):
    hi, lo = split(x)
    xs[c, 0:128] = hi
    xs[c, 128:256] = lo
    xs[c, 256:384] = hi


def product(tile, xs, c):
    hi, lo = split(tile)
    return jnp.dot(
        jnp.concatenate([hi, hi, lo], 1), xs[c], preferred_element_type=jnp.float32
    )


def start_tiles(tiles, buf, sems):
    n = tiles.shape[0] // CHUNKS
    copies = [
        pltpu.make_async_copy(tiles.at[pl.ds(i * n, n)], buf.at[pl.ds(i * n, n)], sems.at[i])
        for i in range(CHUNKS)
    ]
    for c in copies:
        c.start()
    return copies


def place_quarters(rank, pieces, full):
    for k, piece in enumerate(pieces):
        at = lax.rem(rank + 4 - k, 4) * 2
        full[pl.ds(at, 2)] = piece[...]


def take_quarters(rank, full, outs):
    for k, out in enumerate(outs):
        at = lax.rem(rank + k, 4) * 2
        out[...] = full[pl.ds(at, 2)]


def send_blocks(targets, source, outgoing):
    def one(p, _):
        outgoing[p] = source[targets[p]]
        return 0

    lax.fori_loop(0, outgoing.shape[0], one, 0)


def first_kernel(targets, embed, scale, scaled, outgoing):
    scaled[...] = embed[...] * scale[...]
    send_blocks(targets, scaled, outgoing)


def next_kernel(rank, targets, scale, q0, q1, q2, q3, scaled, layer, outgoing):
    place_quarters(rank[0], (q0, q1, q2, q3), scaled)
    s = scale[...]
    cur = scaled[...] * s
    layer[...] = cur
    scaled[...] = cur * s
    send_blocks(targets, scaled, outgoing)


def final_kernel(rank, scale, embed, layer, q0, q1, q2, q3, out):
    place_quarters(rank[0], (q0, q1, q2, q3), out)
    out[...] = (embed[...] + layer[...] + out[...] * scale[...]) / 3.0


def forward_kernel(rank, count, rows, cols, own, arrived, tiles, o0, o1, o2, o3, buf, xs, acc, sems):
    copies = start_tiles(tiles, buf, sems)
    local = own.shape[0]

    def split_own(c, _):
        store_split(xs, c, own[c])
        return 0

    def split_arrived(c, _):
        store_split(xs, local + c, arrived[c])
        return 0

    lax.fori_loop(0, local, split_own, 0)
    lax.fori_loop(0, arrived.shape[0], split_arrived, 0)
    acc[...] = jnp.zeros_like(acc)
    for c in copies:
        c.wait()
    live = count[0]

    def step(i, _):
        prods = [product(buf[i * UNROLL + k], xs, cols[i * UNROLL + k]) for k in range(UNROLL)]
        for k in range(UNROLL):
            t = i * UNROLL + k
            acc[jnp.where(t < live, rows[t], local)] += prods[k]
        return 0

    lax.fori_loop(0, (live + UNROLL - 1) // UNROLL, step, 0)
    take_quarters(rank[0], acc, (o0, o1, o2, o3))


def backward_sums(count, rows, cols, tiles, out_local, out_remote, buf, zs, acc, copies):
    local = out_local.shape[0]
    readable = local + out_remote.shape[0]

    def clear(c, _):
        acc[c] = jnp.zeros(acc.shape[1:], jnp.float32)
        return 0

    lax.fori_loop(0, readable + 1, clear, 0)
    for c in copies:
        c.wait()
    live = count[0]

    def step(i, _):
        prods = [product(buf[i * UNROLL + k].T, zs, rows[i * UNROLL + k]) for k in range(UNROLL)]
        for k in range(UNROLL):
            t = i * UNROLL + k
            acc[jnp.where(t < live, cols[t], readable)] += prods[k]
        return 0

    lax.fori_loop(0, (live + UNROLL - 1) // UNROLL, step, 0)

    def put_local(c, _):
        out_local[c] = acc[c]
        return 0

    def put_remote(c, _):
        out_remote[c] = acc[local + c]
        return 0

    lax.fori_loop(0, local, put_local, 0)
    lax.fori_loop(0, out_remote.shape[0], put_remote, 0)


def backward_first_kernel(count, rows, cols, scale, cot, tiles, out_local, out_remote, buf, zs, acc, sems):
    copies = start_tiles(tiles, buf, sems)

    def prepare(b, _):
        store_split(zs, b, cot[b] / 3.0 * scale[b])
        return 0

    lax.fori_loop(0, cot.shape[0], prepare, 0)
    backward_sums(count, rows, cols, tiles, out_local, out_remote, buf, zs, acc, copies)


def backward_next_kernel(
    rank, count, rows, cols, scale, cot, q0, q1, q2, q3, tiles, out_local, out_remote, buf, zs, acc, sems
):
    copies = start_tiles(tiles, buf, sems)
    place_quarters(rank[0], (q0, q1, q2, q3), acc)

    def prepare(b, _):
        s = scale[b]
        store_split(zs, b, (cot[b] / 3.0 + s * acc[b]) * s)
        return 0

    lax.fori_loop(0, cot.shape[0], prepare, 0)
    backward_sums(count, rows, cols, tiles, out_local, out_remote, buf, zs, acc, copies)


def collect_kernel(rank, targets, local, returned, o0, o1, o2, o3, acc):
    acc[...] = local[...]

    def one(r, _):
        acc[targets[r]] += returned[r]
        return 0

    lax.fori_loop(0, returned.shape[0], one, 0)
    take_quarters(rank[0], acc, (o0, o1, o2, o3))


def adam_kernel(
    rank, scale, cot, embed, first, second, q0, q1, q2, q3, new_embed, new_first, new_second
):
    place_quarters(rank[0], (q0, q1, q2, q3), new_first)

    def one(b, _):
        grad = cot[b] / 3.0 + scale[b] * new_first[b]
        m = 0.9 * first[b] + 0.1 * grad
        v = 0.999 * second[b] + 0.001 * grad * grad
        new_first[b] = m
        new_second[b] = v
        step = m / (1.0 - 0.9**STEP)
        new_embed[b] = embed[b] - 0.01 * step / (jnp.sqrt(v / (1.0 - 0.999**STEP)) + 1e-08)
        return 0

    lax.fori_loop(0, embed.shape[0], one, 0)


def call(kernel, outs, ins, args, us, mib, scratch=()):
    return pl.pallas_call(
        kernel,
        out_shape=outs,
        in_specs=ins,
        out_specs=[VMEM] * len(outs),
        scratch_shapes=scratch,
        compiler_params=params(mib),
        cost_estimate=cost(us),
    )(*args)


def shifted(x, by):
    n = lax.axis_size("grp")
    return lax.ppermute(x, "grp", [(i, (i + by) % n) for i in range(n)])


def sum_and_share(parts):
    own = parts[0] + shifted(parts[1], 1) + shifted(parts[2], 2) + shifted(parts[3], 3)
    return (own, shifted(own, 1), shifted(own, 2), shifted(own, 3))


def exchange(x):
    return lax.all_to_all(x, "dom", split_axis=0, concat_axis=0, tiled=True)


def body(
    embed,
    cotangent,
    first_moment,
    second_moment,
    degrees,
    tiles,
    tile_rows,
    tile_cols,
    tile_count,
    send_list,
):
    block = tiles.shape[-1]
    feature = embed.shape[1]
    local = embed.shape[0] // block
    remote = send_list.shape[1] * send_list.shape[2]
    slots = tiles.shape[2]
    rank = lax.axis_index("grp").astype(jnp.int32).reshape(1)
    scale = (1.0 / jnp.sqrt(degrees.astype(jnp.float32))).reshape(local, block, 1)
    mats = tiles[0, 0]
    rows, cols, count = tile_rows[0, 0], tile_cols[0, 0], tile_count[0]
    targets = send_list.reshape(remote)
    as_blocks = lambda x: x.reshape(local, block, feature)
    emb, cot = as_blocks(embed), as_blocks(cotangent)
    blocks, sent, quarter = f32(local, block, feature), f32(remote, block, feature), f32(2, block, feature)
    quarters = [quarter] * 4
    tile_buf = pltpu.VMEM((slots, block, block), jnp.float32)
    sems = pltpu.SemaphoreType.DMA((CHUNKS,))
    right = lambda n: pltpu.VMEM((n, 3 * block, feature), jnp.bfloat16)
    sums = lambda n: pltpu.VMEM((n, block, feature), jnp.float32)

    def forward(own, arrived):
        return call(
            forward_kernel, quarters, [SMEM] * 4 + [VMEM] * 2 + [ANY],
            (rank, count, rows, cols, own, arrived, mats), 14, 28,
            [tile_buf, right(local + remote), sums(local + 1), sems],
        )

    back_scratch = [tile_buf, right(local), sums(local + remote + 1), sems]
    scaled, outgoing = call(
        first_kernel, [blocks, sent], [SMEM, VMEM, VMEM], (targets, emb, scale), 3, 10
    )
    arrived = exchange(outgoing)
    out_local, out_remote = call(
        backward_first_kernel, [blocks, sent], [SMEM] * 3 + [VMEM] * 2 + [ANY],
        (count, rows, cols, scale, cot, mats), 14, 26, back_scratch,
    )
    returned = exchange(out_remote)
    parts = sum_and_share(forward(scaled, arrived))
    scaled, layer, outgoing = call(
        next_kernel, [blocks, blocks, sent], [SMEM] * 2 + [VMEM] * 5,
        (rank, targets, scale, *parts), 3, 12,
    )
    arrived = exchange(outgoing)
    back = call(
        collect_kernel, quarters, [SMEM] * 2 + [VMEM] * 2,
        (rank, targets, out_local, returned), 3, 10, [sums(local)],
    )
    back = sum_and_share(back)
    out_local, out_remote = call(
        backward_next_kernel, [blocks, sent], [SMEM] * 4 + [VMEM] * 6 + [ANY],
        (rank, count, rows, cols, scale, cot, *back, mats), 14, 26, back_scratch,
    )
    returned = exchange(out_remote)
    parts = sum_and_share(forward(scaled, arrived))
    (final,) = call(
        final_kernel, [blocks], [SMEM] + [VMEM] * 7, (rank, scale, emb, layer, *parts), 2, 10
    )
    back = call(
        collect_kernel, quarters, [SMEM] * 2 + [VMEM] * 2,
        (rank, targets, out_local, returned), 3, 10, [sums(local)],
    )
    back = sum_and_share(back)
    new = call(
        adam_kernel, [blocks] * 3, [SMEM] + [VMEM] * 9,
        (rank, scale, cot, emb, as_blocks(first_moment), as_blocks(second_moment), *back), 4, 14,
    )
    flat = lambda x: x.reshape(local * block, feature)
    return (flat(final), *(flat(x) for x in new))


def solution(mesh):
    in_specs = (
        P("dom", None),
        P("dom", None),
        P("dom", None),
        P("dom", None),
        P("dom"),
        P("dom", "grp", None, None, None),
        P("dom", "grp", None),
        P("dom", "grp", None),
        P("dom", "grp"),
        P("dom", None, None),
    )
    out_specs = (P("dom", None), P("dom", None), P("dom", None), P("dom", None))
    return jax.shard_map(body, mesh=mesh, in_specs=in_specs, out_specs=out_specs, check_vma=False)
```

```python
import functools

import jax
import jax.numpy as jnp
from jax import lax
from jax.experimental import pallas as pl
from jax.experimental.pallas import tpu as pltpu
from jax.sharding import PartitionSpec as P

LAYERS = 2
STEP = 10
CHUNKS = 8
UNROLL = 16
PIECES = 4
EARLY = 2
PLACES = ((0, 0), (0, 1), (1, 0), (3, 1), (1, 1), (3, 0), (2, 0), (2, 1))
QUARTER = 32

SMEM = pl.BlockSpec(memory_space=pltpu.SMEM)
VMEM = pl.BlockSpec(memory_space=pltpu.VMEM)
ANY = pl.BlockSpec(memory_space=pl.ANY)


def f32(*shape):
    return jax.ShapeDtypeStruct(shape, jnp.float32)


def wide(x):
    return jnp.concatenate([x, x], -1)


def split(x):
    hi = x.astype(jnp.bfloat16)
    lo = (x - hi.astype(jnp.float32)).astype(jnp.bfloat16)
    return hi, lo


def store_split(xs, c, x):
    hi, lo = split(x)
    xs[c, 0:128] = hi
    xs[c, 128:256] = lo
    xs[c, 256:384] = hi


def product(tile, xs, c):
    hi, lo = split(tile)
    return jnp.dot(
        jnp.concatenate([hi, hi, lo], 1), xs[c], preferred_element_type=jnp.float32
    )


def copies_of(source, buf, sems, parts):
    n = source.shape[0] // parts
    at = [pl.ds(i * n, n) for i in range(parts)]
    return [pltpu.make_async_copy(source.at[at[i]], buf.at[at[i]], sems.at[i]) for i in range(parts)]


def start(copies):
    for c in copies:
        c.start()


def wait(copies):
    for c in copies:
        c.wait()


def both(x, scale, x_buf, scale_buf, sems):
    copies = [
        pltpu.make_async_copy(x, x_buf, sems.at[CHUNKS]),
        pltpu.make_async_copy(scale, scale_buf, sems.at[CHUNKS + 1]),
    ]
    start(copies)
    return copies


def start_gathered(rank, pieces, buf, sems):
    half = buf.shape[1] // 2
    copies = []
    for i, (piece, (k, part)) in enumerate(zip(pieces, PLACES)):
        at = lax.rem(rank + 4 - k, 4)
        to = buf.at[at, pl.ds(part * half, half)]
        copies.append(pltpu.make_async_copy(piece, to, sems.at[i]))
    start(copies)
    return copies


def rows_of(rank, k):
    return pl.ds(pl.multiple_of(lax.rem(rank + 4 + k, 4) * QUARTER, QUARTER), QUARTER)


def place_quarters(rank, pieces, full):
    for k, piece in enumerate(pieces):
        full[pl.ds(0, piece.shape[0]), rows_of(rank, -k)] = piece[...]


def take_quarters(rank, full, outs):
    for k, out in enumerate(outs):
        out[...] = full[pl.ds(0, out.shape[0]), rows_of(rank, k)]


def send_blocks(targets, source, outgoing):
    def one(p, _):
        outgoing[p] = source[targets[p]]
        return 0

    lax.fori_loop(0, outgoing.shape[0], one, 0, unroll=4)


def first_kernel(rank, targets, embed, scale, outgoing, scaled):
    mine = rows_of(rank[0], 0)
    scaled[...] = embed[:, mine] * wide(scale[:, mine])
    send_blocks(targets, scaled, outgoing)


def next_kernel(rank, targets, scale, p0, p1, p2, p3, outgoing, scaled, sems):
    place_quarters(rank[0], (p0, p1, p2, p3), scaled)

    def one(b, _):
        s = wide(scale[b])
        scaled[b] = scaled[b] * s * s
        return 0

    lax.fori_loop(0, scale.shape[0], one, 0)
    copies = [
        pltpu.make_async_copy(scaled.at[targets[p]], outgoing.at[p], sems.at[p])
        for p in range(outgoing.shape[0])
    ]
    start(copies)
    wait(copies)


def final_kernel(rank, scale, embed, p0, p1, p2, p3, q0, q1, q2, q3, out):
    local = embed.shape[0]
    for k, (p, q) in enumerate(zip((p0, p1, p2, p3), (q0, q1, q2, q3))):
        out[:, rows_of(rank[0], -k)] = p[...] + q[...]

    def one(b, _):
        out[b] = (embed[b] + out[b] * wide(scale[b])) / 3.0
        return 0

    lax.fori_loop(0, local, one, 0)


def split_gathered(gathered, xs, local):
    def one(g, _):
        for j in range(4):
            hi, lo = split(gathered[j, g])
            xs[local + g, j * QUARTER : (j + 1) * QUARTER] = hi
            xs[local + g, 128 + j * QUARTER : 128 + (j + 1) * QUARTER] = lo
            xs[local + g, 256 + j * QUARTER : 256 + (j + 1) * QUARTER] = hi
        return 0

    lax.fori_loop(0, gathered.shape[1], one, 0, unroll=2)


def forward_sums(rank, count, rows, cols, outs, buf, xs, acc, tile_copies, sems):
    local = outs[0].shape[0]
    acc[...] = jnp.zeros_like(acc)

    def step(i, _):
        prods = [product(buf[i * UNROLL + k], xs, cols[i * UNROLL + k]) for k in range(UNROLL)]
        for k in range(UNROLL):
            t = i * UNROLL + k
            acc[jnp.where(t < count[0], rows[t], local)] += prods[k]
        return 0

    in_chunks(count[0], tile_copies, buf.shape[0], step)
    copies = [
        pltpu.make_async_copy(acc.at[pl.ds(0, local), rows_of(rank, k)], out, sems.at[k])
        for k, out in enumerate(outs)
    ]
    start(copies)
    wait(copies)


def in_chunks(live, tile_copies, slots, step):
    steps = (live + UNROLL - 1) // UNROLL
    per = slots // CHUNKS // UNROLL
    for i, copy in enumerate(tile_copies):
        copy.wait()
        lax.fori_loop(i * per, jnp.clip(steps, i * per, (i + 1) * per), step, 0)


def forward_first_kernel(
    rank, count, rows, cols, embed, scale, a0, a1, a2, a3, a4, a5, a6, a7, tiles, o0, o1, o2, o3,
    buf, xs, acc, gathered, sems, more, emb, sc,
):
    local = embed.shape[0]
    first = both(embed, scale, emb, sc, sems)
    copies = start_gathered(rank[0], (a0, a1, a2, a3, a4, a5, a6, a7), gathered, more)
    tile_copies = copies_of(tiles, buf, sems, CHUNKS)
    start(tile_copies[:EARLY])

    wait(first)

    def split_own(c, _):
        store_split(xs, c, emb[c] * wide(sc[c]))
        return 0

    lax.fori_loop(0, local, split_own, 0)
    wait(copies)
    start(tile_copies[EARLY:])
    split_gathered(gathered, xs, local)
    forward_sums(rank[0], count, rows, cols, (o0, o1, o2, o3), buf, xs, acc, tile_copies, sems)


def forward_next_kernel(
    rank, count, rows, cols, scale, p0, p1, p2, p3, arrived, tiles, o0, o1, o2, o3,
    buf, xs, acc, got, sems, more,
):
    local = scale.shape[0]
    copies = copies_of(arrived, got, more, PIECES)
    start(copies)
    tile_copies = copies_of(tiles, buf, sems, CHUNKS)
    start(tile_copies[:EARLY])
    place_quarters(rank[0], (p0, p1, p2, p3), acc)

    def split_own(c, _):
        s = wide(scale[c])
        store_split(xs, c, acc[c] * s * s)
        return 0

    lax.fori_loop(0, local, split_own, 0)
    per = got.shape[0] // PIECES
    for i, copy in enumerate(copies):
        copy.wait()

        def split_arrived(c, _):
            store_split(xs, local + c, got[c])
            return 0

        lax.fori_loop(i * per, (i + 1) * per, split_arrived, 0, unroll=2)
    start(tile_copies[EARLY:])
    forward_sums(rank[0], count, rows, cols, (o0, o1, o2, o3), buf, xs, acc, tile_copies, sems)


def backward_sums(count, rows, cols, buf, zs, acc, tile_copies):
    def clear(c, _):
        acc[c] = jnp.zeros(acc.shape[1:], jnp.float32)
        return 0

    readable = acc.shape[0] - 1
    lax.fori_loop(0, readable, clear, 0, unroll=2)
    start(tile_copies[EARLY:])

    def step(i, _):
        prods = [product(buf[i * UNROLL + k].T, zs, rows[i * UNROLL + k]) for k in range(UNROLL)]
        for k in range(UNROLL):
            t = i * UNROLL + k
            acc[jnp.where(t < count[0], cols[t], readable)] += prods[k]
        return 0

    in_chunks(count[0], tile_copies, buf.shape[0], step)


def backward_first_kernel(
    count, rows, cols, scale, cot, tiles, out_local, out_remote, buf, zs, acc, sems, more, ct, sc
):
    local, remote = out_local.shape[0], out_remote.shape[0]
    first = both(cot, scale, ct, sc, sems)
    tile_copies = copies_of(tiles, buf, sems, CHUNKS)
    start(tile_copies[:EARLY])

    wait(first)

    def prepare(b, _):
        store_split(zs, b, ct[b] / 3.0 * wide(sc[b]))
        return 0

    lax.fori_loop(0, local, prepare, 0)
    backward_sums(count, rows, cols, buf, zs, acc, tile_copies)
    copies = [
        pltpu.make_async_copy(acc.at[pl.ds(local, remote)], out_remote, more.at[0]),
        pltpu.make_async_copy(acc.at[pl.ds(0, local)], out_local, more.at[1]),
    ]
    start(copies)
    wait(copies)


def backward_next_kernel(
    rank, count, rows, cols, scale, cot, q0, q1, q2, q3, tiles, o0, o1, o2, o3, o4, o5, o6, o7,
    buf, zs, acc, sems, more, ct, sc,
):
    first = both(cot, scale, ct, sc, sems)
    tile_copies = copies_of(tiles, buf, sems, CHUNKS)
    start(tile_copies[:EARLY])
    place_quarters(rank[0], (q0, q1, q2, q3), acc)
    wait(first)

    def prepare(b, _):
        s = wide(sc[b])
        store_split(zs, b, (ct[b] / 3.0 + s * acc[b]) * s)
        return 0

    lax.fori_loop(0, cot.shape[0], prepare, 0)
    backward_sums(count, rows, cols, buf, zs, acc, tile_copies)
    half = o0.shape[0]
    copies = []
    for i, out in enumerate((o0, o1, o2, o3, o4, o5, o6, o7)):
        source = acc.at[pl.ds(i % 2 * half, half), rows_of(rank[0], i // 2)]
        copies.append(pltpu.make_async_copy(source, out, more.at[i]))
    start(copies)
    wait(copies)


def own_rows_kernel(targets, local, returned, out):
    out[...] = local[...]

    def one(r, _):
        out[targets[r]] += returned[r]
        return 0

    lax.fori_loop(0, returned.shape[0], one, 0, unroll=2)


def collect_kernel(rank, targets, local, returned, after, o0, o1, o2, o3, acc, got, sems):
    own = pltpu.make_async_copy(local, acc, sems.at[PIECES])
    own.start()
    copies = copies_of(returned, got, sems, PIECES)
    start(copies)
    own.wait()
    per = got.shape[0] // PIECES
    for i, copy in enumerate(copies):
        copy.wait()

        def one(r, _, i=i):
            acc[targets[i * per + r]] += got[i * per + r]
            return 0

        lax.fori_loop(0, per, one, 0, unroll=2)
    take_quarters(rank[0], acc, (o0, o1, o2, o3))


def adam_kernel(
    rank, scale, cot, embed, first, second, q0, q1, q2, q3, new_embed, new_first, new_second
):
    place_quarters(rank[0], (q0, q1, q2, q3), new_first)

    def one(b, _):
        grad = cot[b] / 3.0 + wide(scale[b]) * new_first[b]
        m = 0.9 * first[b] + 0.1 * grad
        v = 0.999 * second[b] + 0.001 * grad * grad
        new_first[b] = m
        new_second[b] = v
        step = m / (1.0 - 0.9**STEP)
        new_embed[b] = embed[b] - 0.01 * step / (jnp.sqrt(v / (1.0 - 0.999**STEP)) + 1e-08)
        return 0

    lax.fori_loop(0, embed.shape[0], one, 0)


def call(kernel, outs, ins, args, us, scratch=(), out_spec=VMEM, mib=60):
    return pl.pallas_call(
        kernel,
        out_shape=outs,
        in_specs=ins,
        out_specs=[out_spec] * len(outs),
        scratch_shapes=scratch,
        compiler_params=pltpu.CompilerParams(vmem_limit_bytes=mib * 2**20),
        cost_estimate=pl.CostEstimate(flops=0, bytes_accessed=int(us * 3.6e6), transcendentals=0),
    )(*args)


def shifted(x, by):
    n = lax.axis_size("grp")
    return lax.ppermute(x, "grp", [(i, (i + by) % n) for i in range(n)])


def helper_sum(parts):
    return parts[0] + shifted(parts[1], 1) + shifted(parts[2], 2) + shifted(parts[3], 3)


def shared(own):
    return (own, shifted(own, 1), shifted(own, 2), shifted(own, 3))


def spread(low, high):
    a1, c2 = shifted(low, 1), shifted(high, 3)
    a2, c1 = shifted(high, 1), shifted(low, 3)
    return (low, high, a1, c2, a2, c1, shifted(a1, 1), shifted(c2, 3))


def combine(parts):
    own_low, own_high, up_low, up_high, far_low, far_high, down_low, down_high = parts
    via_up, via_down = shifted(far_low, 1), shifted(far_high, 3)
    got_high, got_low = shifted(up_high, 1), shifted(down_low, 3)
    last_low, last_high = shifted(up_low + via_up, 1), shifted(down_high + via_down, 3)
    return (own_low, got_low, last_low), (own_high, got_high, last_high)


def after(x, y):
    return lax.optimization_barrier((x, y))[0]


def exchange(x):
    return lax.all_to_all(x, "dom", split_axis=0, concat_axis=0, tiled=True)


def body(
    embed,
    cotangent,
    first_moment,
    second_moment,
    degrees,
    tiles,
    tile_rows,
    tile_cols,
    tile_count,
    send_list,
):
    block = tiles.shape[-1]
    feature = embed.shape[1]
    local = embed.shape[0] // block
    remote = send_list.shape[1] * send_list.shape[2]
    slots = tiles.shape[2]
    rank = lax.axis_index("grp").astype(jnp.int32).reshape(1)
    scale = 1.0 / jnp.sqrt(degrees.astype(jnp.float32))
    scale = jnp.broadcast_to(scale.reshape(local, block, 1), (local, block, 128))
    mats = tiles[0, 0]
    rows, cols, count = tile_rows[0, 0], tile_cols[0, 0], tile_count[0]
    targets = send_list.reshape(remote)
    as_blocks = lambda x: x.reshape(local, block, feature)
    emb, cot = as_blocks(embed), as_blocks(cotangent)
    blocks, sent = f32(local, block, feature), f32(remote, block, feature)
    sent_rows = f32(remote, QUARTER, feature)
    quarters = [f32(local, QUARTER, feature)] * 4
    tile_buf = pltpu.VMEM((slots, block, block), jnp.float32)
    sems = lambda n: pltpu.SemaphoreType.DMA((n,))
    right = lambda n: pltpu.VMEM((n, 3 * block, feature), jnp.bfloat16)
    sums = lambda n: pltpu.VMEM((n, block, feature), jnp.float32)
    some_rows = pltpu.VMEM((local, QUARTER, feature), jnp.float32)
    fwd_scratch = lambda got, n: [
        tile_buf, right(local + remote), sums(local + 1), pltpu.VMEM(got, jnp.float32),
        sems(CHUNKS + 2), sems(n),
    ]
    two = [sums(local), pltpu.VMEM((local, block, 128), jnp.float32)]
    back_scratch = lambda n: [tile_buf, right(local), sums(local + remote + 1), sems(CHUNKS + 2), sems(n), *two]

    (outgoing,) = call(
        first_kernel, [sent_rows], [SMEM] * 2 + [VMEM] * 2, (rank, targets, emb, scale), 2, [some_rows], mib=8
    )
    arrived = exchange(outgoing)
    out_local, out_remote = call(
        backward_first_kernel, [blocks, sent], [SMEM] * 3 + [ANY] * 3,
        (count, rows, cols, scale, cot, mats), 10, back_scratch(2), ANY,
    )
    arrived = after(arrived, out_remote)
    arrived = spread(arrived[: remote // 2], arrived[remote // 2 :])
    returned = exchange(out_remote)
    parts = call(
        forward_first_kernel, quarters, [SMEM] * 4 + [ANY] * 11,
        (rank, count, rows, cols, emb, scale, *arrived, mats), 10,
        fwd_scratch((4, remote, QUARTER, feature), len(PLACES)) + two, ANY,
    )
    collect_scratch = [sums(local), sums(remote), sems(PIECES + 1)]
    back = call(
        collect_kernel, quarters, [SMEM] * 2 + [ANY] * 3,
        (rank, targets, out_local, returned, parts[0]), 4, collect_scratch, mib=14,
    )
    parts, back = lax.optimization_barrier((parts, back))
    back = shared(helper_sum(back))
    layer = shared(helper_sum(parts))
    (outgoing,) = call(
        next_kernel, [sent], [SMEM] * 2 + [VMEM] * 5, (rank, targets, scale, after(layer[0], back), *layer[1:]), 3,
        [sums(local), sems(remote)], ANY,
    )
    arrived = exchange(outgoing)
    half = (local + remote) // 2
    back = call(
        backward_next_kernel, [f32(half, QUARTER, feature)] * 8, [SMEM] * 4 + [ANY] * 2 + [VMEM] * 4 + [ANY],
        (rank, count, rows, cols, scale, cot, *back, mats), 10, back_scratch(8), ANY,
    )
    low, high = combine(back)
    parts = call(
        forward_next_kernel, quarters, [SMEM] * 4 + [VMEM] * 5 + [ANY] * 2,
        (rank, count, rows, cols, scale, *layer, arrived, mats), 10,
        fwd_scratch((remote, block, feature), PIECES), ANY,
    )
    low, high = low[0] + low[1] + after(low[2], parts[0]), high[0] + high[1] + high[2]
    own = low[:local]
    outgoing = jnp.concatenate([low[local:], high], 0)
    returned = exchange(outgoing)
    parts = shared(helper_sum(parts))
    (final,) = call(
        final_kernel, [blocks], [SMEM] + [VMEM] * 10, (rank, scale, emb, *layer, *parts), 3, mib=10
    )
    (back,) = call(own_rows_kernel, quarters[:1], [SMEM] + [VMEM] * 2, (targets, own, returned), 2, mib=8)
    back = shared(back)
    new = call(
        adam_kernel, [blocks] * 3, [SMEM] + [VMEM] * 9,
        (rank, scale, cot, emb, as_blocks(first_moment), as_blocks(second_moment), *back), 4, mib=14,
    )
    flat = lambda x: x.reshape(local * block, feature)
    return (flat(final), *(flat(x) for x in new))


def solution(mesh):
    in_specs = (
        P("dom", None),
        P("dom", None),
        P("dom", None),
        P("dom", None),
        P("dom"),
        P("dom", "grp", None, None, None),
        P("dom", "grp", None),
        P("dom", "grp", None),
        P("dom", "grp"),
        P("dom", None, None),
    )
    out_specs = (P("dom", None), P("dom", None), P("dom", None), P("dom", None))
    return jax.shard_map(body, mesh=mesh, in_specs=in_specs, out_specs=out_specs, check_vma=False)
```

```python
import functools

import jax
import jax.numpy as jnp
from jax import lax
from jax.experimental import pallas as pl
from jax.experimental.pallas import tpu as pltpu
from jax.sharding import PartitionSpec as P

LAYERS = 2
STEP = 10
CHUNKS = 8
UNROLL = 16
PIECES = 4
EARLY = 2
PLACES = ((0, 0), (0, 1), (1, 0), (3, 1), (1, 1), (3, 0), (2, 0), (2, 1))
QUARTER = 32

SMEM = pl.BlockSpec(memory_space=pltpu.SMEM)
VMEM = pl.BlockSpec(memory_space=pltpu.VMEM)
ANY = pl.BlockSpec(memory_space=pl.ANY)


def f32(*shape):
    return jax.ShapeDtypeStruct(shape, jnp.float32)


def wide(x):
    return jnp.concatenate([x, x], -1)


def split(x):
    hi = x.astype(jnp.bfloat16)
    lo = (x - hi.astype(jnp.float32)).astype(jnp.bfloat16)
    return hi, lo


def store_split(xs, c, x):
    hi, lo = split(x)
    xs[c, 0:128] = hi
    xs[c, 128:256] = lo
    xs[c, 256:384] = hi


def product(tile, xs, c):
    hi, lo = split(tile)
    return jnp.dot(
        jnp.concatenate([hi, hi, lo], 1), xs[c], preferred_element_type=jnp.float32
    )


def copies_of(source, buf, sems, parts):
    n = source.shape[0] // parts
    at = [pl.ds(i * n, n) for i in range(parts)]
    return [pltpu.make_async_copy(source.at[at[i]], buf.at[at[i]], sems.at[i]) for i in range(parts)]


def start(copies):
    for c in copies:
        c.start()


def wait(copies):
    for c in copies:
        c.wait()


def both(x, scale, x_buf, scale_buf, sems):
    copies = [
        pltpu.make_async_copy(x, x_buf, sems.at[CHUNKS]),
        pltpu.make_async_copy(scale, scale_buf, sems.at[CHUNKS + 1]),
    ]
    start(copies)
    return copies


def start_gathered(rank, pieces, buf, sems):
    half = buf.shape[1] // 2
    copies = []
    for i, (piece, (k, part)) in enumerate(zip(pieces, PLACES)):
        at = lax.rem(rank + 4 - k, 4)
        to = buf.at[at, pl.ds(part * half, half)]
        copies.append(pltpu.make_async_copy(piece, to, sems.at[i]))
    start(copies)
    return copies


def rows_of(rank, k):
    return pl.ds(pl.multiple_of(lax.rem(rank + 4 + k, 4) * QUARTER, QUARTER), QUARTER)


def place_quarters(rank, pieces, full):
    for k, piece in enumerate(pieces):
        full[pl.ds(0, piece.shape[0]), rows_of(rank, -k)] = piece[...]


def take_quarters(rank, full, outs):
    for k, out in enumerate(outs):
        out[...] = full[pl.ds(0, out.shape[0]), rows_of(rank, k)]


def send_blocks(targets, source, outgoing):
    def one(p, _):
        outgoing[p] = source[targets[p]]
        return 0

    lax.fori_loop(0, outgoing.shape[0], one, 0, unroll=4)


def first_kernel(rank, targets, embed, scale, outgoing, scaled):
    mine = rows_of(rank[0], 0)
    scaled[...] = embed[:, mine] * wide(scale[:, mine])
    send_blocks(targets, scaled, outgoing)


def next_kernel(rank, targets, scale, p0, p1, p2, p3, outgoing, scaled, sems):
    place_quarters(rank[0], (p0, p1, p2, p3), scaled)

    def one(b, _):
        s = wide(scale[b])
        scaled[b] = scaled[b] * s * s
        return 0

    lax.fori_loop(0, scale.shape[0], one, 0)
    copies = [
        pltpu.make_async_copy(scaled.at[targets[p]], outgoing.at[p], sems.at[p])
        for p in range(outgoing.shape[0])
    ]
    start(copies)
    wait(copies)


def final_kernel(rank, scale, embed, p0, p1, p2, p3, q0, q1, q2, q3, out):
    local = embed.shape[0]
    for k, (p, q) in enumerate(zip((p0, p1, p2, p3), (q0, q1, q2, q3))):
        out[:, rows_of(rank[0], -k)] = p[...] + q[...]

    def one(b, _):
        out[b] = (embed[b] + out[b] * wide(scale[b])) / 3.0
        return 0

    lax.fori_loop(0, local, one, 0)


def split_piece(rank, place, gathered, xs, local):
    k, part = place
    j = lax.rem(rank + 4 - k, 4)
    half = gathered.shape[1] // 2
    row = pl.multiple_of(j * QUARTER, QUARTER)

    def one(g, _):
        hi, lo = split(gathered[j, g])
        xs[local + g, pl.ds(row, QUARTER)] = hi
        xs[local + g, pl.ds(row + 128, QUARTER)] = lo
        xs[local + g, pl.ds(row + 256, QUARTER)] = hi
        return 0

    lax.fori_loop(part * half, (part + 1) * half, one, 0, unroll=4)


def forward_sums(rank, count, rows, cols, outs, buf, xs, acc, tile_copies, sems):
    local = outs[0].shape[0]

    def step(i, _):
        prods = [product(buf[i * UNROLL + k], xs, cols[i * UNROLL + k]) for k in range(UNROLL)]
        for k in range(UNROLL):
            t = i * UNROLL + k
            acc[jnp.where(t < count[0], rows[t], local)] += prods[k]
        return 0

    in_chunks(count[0], tile_copies, buf.shape[0], step)
    copies = [
        pltpu.make_async_copy(acc.at[pl.ds(0, local), rows_of(rank, k)], out, sems.at[k])
        for k, out in enumerate(outs)
    ]
    start(copies)
    wait(copies)


def in_chunks(live, tile_copies, slots, step):
    steps = (live + UNROLL - 1) // UNROLL
    per = slots // CHUNKS // UNROLL
    for i, copy in enumerate(tile_copies):
        copy.wait()
        lax.fori_loop(i * per, jnp.clip(steps, i * per, (i + 1) * per), step, 0)


def forward_first_kernel(
    rank, count, rows, cols, embed, scale, a0, a1, a2, a3, a4, a5, a6, a7, tiles, o0, o1, o2, o3,
    buf, xs, acc, gathered, sems, more, emb, sc,
):
    local = embed.shape[0]
    first = both(embed, scale, emb, sc, sems)
    copies = start_gathered(rank[0], (a0, a1, a2, a3, a4, a5, a6, a7), gathered, more)
    tile_copies = copies_of(tiles, buf, sems, CHUNKS)
    start(tile_copies[:EARLY])

    acc[...] = jnp.zeros_like(acc)
    wait(first)

    def split_own(c, _):
        store_split(xs, c, emb[c] * wide(sc[c]))
        return 0

    lax.fori_loop(0, local, split_own, 0)
    for place, copy in zip(PLACES, copies):
        copy.wait()
        split_piece(rank[0], place, gathered, xs, local)
    start(tile_copies[EARLY:])
    forward_sums(rank[0], count, rows, cols, (o0, o1, o2, o3), buf, xs, acc, tile_copies, sems)


def forward_next_kernel(
    rank, count, rows, cols, scale, p0, p1, p2, p3, arrived, tiles, o0, o1, o2, o3,
    buf, xs, acc, got, sems, more,
):
    local = scale.shape[0]
    copies = copies_of(arrived, got, more, PIECES)
    start(copies)
    tile_copies = copies_of(tiles, buf, sems, CHUNKS)
    start(tile_copies[:EARLY])
    place_quarters(rank[0], (p0, p1, p2, p3), acc)

    def split_own(c, _):
        s = wide(scale[c])
        store_split(xs, c, acc[c] * s * s)
        return 0

    lax.fori_loop(0, local, split_own, 0)
    acc[...] = jnp.zeros_like(acc)
    per = got.shape[0] // PIECES
    for i, copy in enumerate(copies):
        copy.wait()

        def split_arrived(c, _):
            store_split(xs, local + c, got[c])
            return 0

        lax.fori_loop(i * per, (i + 1) * per, split_arrived, 0, unroll=2)
    start(tile_copies[EARLY:])
    forward_sums(rank[0], count, rows, cols, (o0, o1, o2, o3), buf, xs, acc, tile_copies, sems)


def clear(acc, begin):
    def one(c, _):
        acc[c] = jnp.zeros(acc.shape[1:], jnp.float32)
        return 0

    lax.fori_loop(begin, acc.shape[0] - 1, one, 0, unroll=2)


def backward_sums(count, rows, cols, buf, zs, acc, tile_copies):
    readable = acc.shape[0] - 1
    start(tile_copies[EARLY:])

    def step(i, _):
        prods = [product(buf[i * UNROLL + k].T, zs, rows[i * UNROLL + k]) for k in range(UNROLL)]
        for k in range(UNROLL):
            t = i * UNROLL + k
            acc[jnp.where(t < count[0], cols[t], readable)] += prods[k]
        return 0

    in_chunks(count[0], tile_copies, buf.shape[0], step)


def backward_first_kernel(
    count, rows, cols, scale, cot, tiles, out_local, out_remote, buf, zs, acc, sems, more, ct, sc
):
    local, remote = out_local.shape[0], out_remote.shape[0]
    first = both(cot, scale, ct, sc, sems)
    tile_copies = copies_of(tiles, buf, sems, CHUNKS)
    start(tile_copies[:EARLY])

    clear(acc, 0)
    wait(first)

    def prepare(b, _):
        store_split(zs, b, ct[b] / 3.0 * wide(sc[b]))
        return 0

    lax.fori_loop(0, local, prepare, 0)
    backward_sums(count, rows, cols, buf, zs, acc, tile_copies)
    copies = [
        pltpu.make_async_copy(acc.at[pl.ds(local, remote)], out_remote, more.at[0]),
        pltpu.make_async_copy(acc.at[pl.ds(0, local)], out_local, more.at[1]),
    ]
    start(copies)
    wait(copies)


def backward_next_kernel(
    rank, count, rows, cols, scale, cot, q0, q1, q2, q3, tiles, o0, o1, o2, o3, o4, o5, o6, o7,
    buf, zs, acc, sems, more, ct, sc,
):
    first = both(cot, scale, ct, sc, sems)
    tile_copies = copies_of(tiles, buf, sems, CHUNKS)
    start(tile_copies[:EARLY])
    clear(acc, cot.shape[0])
    place_quarters(rank[0], (q0, q1, q2, q3), acc)
    wait(first)

    def prepare(b, _):
        s = wide(sc[b])
        store_split(zs, b, (ct[b] / 3.0 + s * acc[b]) * s)
        acc[b] = jnp.zeros(acc.shape[1:], jnp.float32)
        return 0

    lax.fori_loop(0, cot.shape[0], prepare, 0)
    backward_sums(count, rows, cols, buf, zs, acc, tile_copies)
    half = o0.shape[0]
    copies = []
    for i, out in enumerate((o0, o1, o2, o3, o4, o5, o6, o7)):
        source = acc.at[pl.ds(i % 2 * half, half), rows_of(rank[0], i // 2)]
        copies.append(pltpu.make_async_copy(source, out, more.at[i]))
    start(copies)
    wait(copies)


def own_rows_kernel(targets, local, returned, out):
    out[...] = local[...]

    def one(r, _):
        out[targets[r]] += returned[r]
        return 0

    lax.fori_loop(0, returned.shape[0], one, 0, unroll=2)


def collect_kernel(rank, targets, local, returned, after, o0, o1, o2, o3, acc, got, sems):
    own = pltpu.make_async_copy(local, acc, sems.at[PIECES])
    own.start()
    copies = copies_of(returned, got, sems, PIECES)
    start(copies)
    own.wait()
    per = got.shape[0] // PIECES
    for i, copy in enumerate(copies):
        copy.wait()

        def one(r, _, i=i):
            acc[targets[i * per + r]] += got[i * per + r]
            return 0

        lax.fori_loop(0, per, one, 0, unroll=2)
    take_quarters(rank[0], acc, (o0, o1, o2, o3))


def adam_kernel(
    rank, scale, cot, embed, first, second, q0, q1, q2, q3, new_embed, new_first, new_second
):
    place_quarters(rank[0], (q0, q1, q2, q3), new_first)

    def one(b, _):
        grad = cot[b] / 3.0 + wide(scale[b]) * new_first[b]
        m = 0.9 * first[b] + 0.1 * grad
        v = 0.999 * second[b] + 0.001 * grad * grad
        new_first[b] = m
        new_second[b] = v
        step = m / (1.0 - 0.9**STEP)
        new_embed[b] = embed[b] - 0.01 * step / (jnp.sqrt(v / (1.0 - 0.999**STEP)) + 1e-08)
        return 0

    lax.fori_loop(0, embed.shape[0], one, 0)


def call(kernel, outs, ins, args, us, scratch=(), out_spec=VMEM, mib=60):
    return pl.pallas_call(
        kernel,
        out_shape=outs,
        in_specs=ins,
        out_specs=[out_spec] * len(outs),
        scratch_shapes=scratch,
        compiler_params=pltpu.CompilerParams(vmem_limit_bytes=mib * 2**20),
        cost_estimate=pl.CostEstimate(flops=0, bytes_accessed=int(us * 3.6e6), transcendentals=0),
    )(*args)


def shifted(x, by):
    n = lax.axis_size("grp")
    return lax.ppermute(x, "grp", [(i, (i + by) % n) for i in range(n)])


def helper_sum(parts):
    return parts[0] + shifted(parts[1], 1) + shifted(parts[2], 2) + shifted(parts[3], 3)


def shared(own):
    return (own, shifted(own, 1), shifted(own, 2), shifted(own, 3))


def spread(low, high):
    a1, c2 = shifted(low, 1), shifted(high, 3)
    a2, c1 = shifted(high, 1), shifted(low, 3)
    return (low, high, a1, c2, a2, c1, shifted(a1, 1), shifted(c2, 3))


def combine(parts):
    own_low, own_high, up_low, up_high, far_low, far_high, down_low, down_high = parts
    via_up, via_down = shifted(far_low, 1), shifted(far_high, 3)
    got_high, got_low = shifted(up_high, 1), shifted(down_low, 3)
    last_low, last_high = shifted(up_low + via_up, 1), shifted(down_high + via_down, 3)
    return (own_low, got_low, last_low), (own_high, got_high, last_high)


def after(x, y):
    return lax.optimization_barrier((x, y))[0]


def exchange(x):
    return lax.all_to_all(x, "dom", split_axis=0, concat_axis=0, tiled=True)


def body(
    embed,
    cotangent,
    first_moment,
    second_moment,
    degrees,
    tiles,
    tile_rows,
    tile_cols,
    tile_count,
    send_list,
):
    block = tiles.shape[-1]
    feature = embed.shape[1]
    local = embed.shape[0] // block
    remote = send_list.shape[1] * send_list.shape[2]
    slots = tiles.shape[2]
    rank = lax.axis_index("grp").astype(jnp.int32).reshape(1)
    scale = 1.0 / jnp.sqrt(degrees.astype(jnp.float32))
    scale = jnp.broadcast_to(scale.reshape(local, block, 1), (local, block, 128))
    mats = tiles[0, 0]
    rows, cols, count = tile_rows[0, 0], tile_cols[0, 0], tile_count[0]
    targets = send_list.reshape(remote)
    as_blocks = lambda x: x.reshape(local, block, feature)
    emb, cot = as_blocks(embed), as_blocks(cotangent)
    blocks, sent = f32(local, block, feature), f32(remote, block, feature)
    sent_rows = f32(remote, QUARTER, feature)
    quarters = [f32(local, QUARTER, feature)] * 4
    tile_buf = pltpu.VMEM((slots, block, block), jnp.float32)
    sems = lambda n: pltpu.SemaphoreType.DMA((n,))
    right = lambda n: pltpu.VMEM((n, 3 * block, feature), jnp.bfloat16)
    sums = lambda n: pltpu.VMEM((n, block, feature), jnp.float32)
    some_rows = pltpu.VMEM((local, QUARTER, feature), jnp.float32)
    fwd_scratch = lambda got, n: [
        tile_buf, right(local + remote), sums(local + 1), pltpu.VMEM(got, jnp.float32),
        sems(CHUNKS + 2), sems(n),
    ]
    two = [sums(local), pltpu.VMEM((local, block, 128), jnp.float32)]
    back_scratch = lambda n: [tile_buf, right(local), sums(local + remote + 1), sems(CHUNKS + 2), sems(n), *two]

    (outgoing,) = call(
        first_kernel, [sent_rows], [SMEM] * 2 + [VMEM] * 2, (rank, targets, emb, scale), 2, [some_rows], mib=8
    )
    arrived = exchange(outgoing)
    out_local, out_remote = call(
        backward_first_kernel, [blocks, sent], [SMEM] * 3 + [ANY] * 3,
        (count, rows, cols, scale, cot, mats), 10, back_scratch(2), ANY,
    )
    arrived = after(arrived, out_remote)
    arrived = spread(arrived[: remote // 2], arrived[remote // 2 :])
    parts = call(
        forward_first_kernel, quarters, [SMEM] * 4 + [ANY] * 11,
        (rank, count, rows, cols, emb, scale, *arrived, mats), 10,
        fwd_scratch((4, remote, QUARTER, feature), len(PLACES)) + two, ANY,
    )
    returned = exchange(out_remote)
    collect_scratch = [sums(local), sums(remote), sems(PIECES + 1)]

    def collect(local_sums, returned, after_this):
        return call(
            collect_kernel, quarters, [SMEM] * 2 + [ANY] * 3,
            (rank, targets, local_sums, returned, after_this), 4, collect_scratch, mib=14,
        )

    back = collect(out_local, returned, parts[0])
    parts, back = lax.optimization_barrier((parts, back))
    back = shared(helper_sum(back))
    layer = shared(helper_sum(parts))
    half = (local + remote) // 2
    back = call(
        backward_next_kernel, [f32(half, QUARTER, feature)] * 8, [SMEM] * 4 + [ANY] * 2 + [VMEM] * 4 + [ANY],
        (rank, count, rows, cols, scale, cot, *back, mats), 10, back_scratch(8), ANY,
    )
    first = after(layer[0], back[0])
    low, high = combine(back)
    (outgoing,) = call(
        next_kernel, [sent], [SMEM] * 2 + [VMEM] * 5, (rank, targets, scale, first, *layer[1:]), 3,
        [sums(local), sems(remote)], ANY,
    )
    arrived = exchange(outgoing)
    parts = call(
        forward_next_kernel, quarters, [SMEM] * 4 + [VMEM] * 5 + [ANY] * 2,
        (rank, count, rows, cols, scale, *layer, arrived, mats), 10,
        fwd_scratch((remote, block, feature), PIECES), ANY,
    )
    low, high = low[0] + low[1] + low[2], high[0] + high[1] + high[2]
    own = low[:local]
    returned = exchange(jnp.concatenate([low[local:], high], 0))
    (back,) = call(own_rows_kernel, quarters[:1], [SMEM] + [VMEM] * 2, (targets, own, returned), 2, mib=8)
    parts = [parts[0]] + [shifted(parts[k], k) for k in (1, 2, 3)]
    parts = shared(parts[0] + after(parts[1], back) + parts[2] + parts[3])
    base = after(emb, back)
    (final,) = call(
        final_kernel, [blocks], [SMEM] + [VMEM] * 10, (rank, scale, base, *layer, *parts), 3, mib=10
    )
    back = shared(back)
    new = call(
        adam_kernel, [blocks] * 3, [SMEM] + [VMEM] * 9,
        (rank, scale, cot, emb, as_blocks(first_moment), as_blocks(second_moment), *back), 4, mib=14,
    )
    flat = lambda x: x.reshape(local * block, feature)
    return (flat(final), *(flat(x) for x in new))


def solution(mesh):
    in_specs = (
        P("dom", None),
        P("dom", None),
        P("dom", None),
        P("dom", None),
        P("dom"),
        P("dom", "grp", None, None, None),
        P("dom", "grp", None),
        P("dom", "grp", None),
        P("dom", "grp"),
        P("dom", None, None),
    )
    out_specs = (P("dom", None), P("dom", None), P("dom", None), P("dom", None))
    return jax.shard_map(body, mesh=mesh, in_specs=in_specs, out_specs=out_specs, check_vma=False)
```

```python
import functools

import jax
import jax.numpy as jnp
from jax import lax
from jax.experimental import pallas as pl
from jax.experimental.pallas import tpu as pltpu
from jax.sharding import PartitionSpec as P

LAYERS = 2
STEP = 10
CHUNKS = 4
UNROLL = 32
PIECES = 4
EARLY = 1
PLACES = ((0, 0), (0, 1), (1, 0), (3, 1), (1, 1), (3, 0), (2, 0), (2, 1))
QUARTER = 32

SMEM = pl.BlockSpec(memory_space=pltpu.SMEM)
VMEM = pl.BlockSpec(memory_space=pltpu.VMEM)
ANY = pl.BlockSpec(memory_space=pl.ANY)


def f32(*shape):
    return jax.ShapeDtypeStruct(shape, jnp.float32)


def wide(x):
    return jnp.concatenate([x, x], -1)


def split(x):
    hi = x.astype(jnp.bfloat16)
    lo = (x - hi.astype(jnp.float32)).astype(jnp.bfloat16)
    return hi, lo


def store_split(xs, c, x):
    hi, lo = split(x)
    xs[c, 0:128] = hi
    xs[c, 128:256] = lo


def product(tile, xs, c):
    hi, lo = split(tile)
    both_hi = jnp.dot(jnp.concatenate([hi, hi], 1), xs[c], preferred_element_type=jnp.float32)
    return both_hi + jnp.dot(lo, xs[c, 0:128], preferred_element_type=jnp.float32)


def copies_of(source, buf, sems, parts):
    n = source.shape[0] // parts
    at = [pl.ds(i * n, n) for i in range(parts)]
    return [pltpu.make_async_copy(source.at[at[i]], buf.at[at[i]], sems.at[i]) for i in range(parts)]


def start(copies):
    for c in copies:
        c.start()


def wait(copies):
    for c in copies:
        c.wait()


def both(x, scale, x_buf, scale_buf, sems):
    copies = [
        pltpu.make_async_copy(x, x_buf, sems.at[CHUNKS]),
        pltpu.make_async_copy(scale, scale_buf, sems.at[CHUNKS + 1]),
    ]
    start(copies)
    return copies


def start_gathered(rank, pieces, buf, sems):
    half = buf.shape[1] // 2
    copies = []
    for i, (piece, (k, part)) in enumerate(zip(pieces, PLACES)):
        at = lax.rem(rank + 4 - k, 4)
        to = buf.at[at, pl.ds(part * half, half)]
        copies.append(pltpu.make_async_copy(piece, to, sems.at[i]))
    start(copies)
    return copies


def rows_of(rank, k):
    return pl.ds(pl.multiple_of(lax.rem(rank + 4 + k, 4) * QUARTER, QUARTER), QUARTER)


def place_quarters(rank, pieces, full):
    for k, piece in enumerate(pieces):
        full[pl.ds(0, piece.shape[0]), rows_of(rank, -k)] = piece[...]


def take_quarters(rank, full, outs):
    for k, out in enumerate(outs):
        out[...] = full[pl.ds(0, out.shape[0]), rows_of(rank, k)]


def send_blocks(targets, source, outgoing):
    def one(p, _):
        outgoing[p] = source[targets[p]]
        return 0

    lax.fori_loop(0, outgoing.shape[0], one, 0, unroll=4)


def first_kernel(rank, targets, embed, scale, outgoing, scaled):
    mine = rows_of(rank[0], 0)
    scaled[...] = embed[:, mine] * wide(scale[:, mine])
    send_blocks(targets, scaled, outgoing)


def next_kernel(rank, targets, scale, p0, p1, p2, p3, outgoing, scaled, sems):
    place_quarters(rank[0], (p0, p1, p2, p3), scaled)

    def one(b, _):
        s = wide(scale[b])
        scaled[b] = scaled[b] * s * s
        return 0

    lax.fori_loop(0, scale.shape[0], one, 0)
    copies = [
        pltpu.make_async_copy(scaled.at[targets[p]], outgoing.at[p], sems.at[p])
        for p in range(outgoing.shape[0])
    ]
    start(copies)
    wait(copies)


def final_kernel(rank, scale, embed, p0, p1, p2, p3, q0, q1, q2, q3, out):
    local = embed.shape[0]
    for k, (p, q) in enumerate(zip((p0, p1, p2, p3), (q0, q1, q2, q3))):
        out[:, rows_of(rank[0], -k)] = p[...] + q[...]

    def one(b, _):
        out[b] = (embed[b] + out[b] * wide(scale[b])) / 3.0
        return 0

    lax.fori_loop(0, local, one, 0)


def split_piece(rank, place, gathered, xs, local):
    k, part = place
    j = lax.rem(rank + 4 - k, 4)
    half = gathered.shape[1] // 2
    row = pl.multiple_of(j * QUARTER, QUARTER)

    def one(g, _):
        hi, lo = split(gathered[j, g])
        xs[local + g, pl.ds(row, QUARTER)] = hi
        xs[local + g, pl.ds(row + 128, QUARTER)] = lo
        return 0

    lax.fori_loop(part * half, (part + 1) * half, one, 0, unroll=4)


def forward_sums(rank, count, rows, cols, outs, buf, xs, acc, tile_copies, sems):
    local = outs[0].shape[0]

    def step(i, _):
        prods = [product(buf[i * UNROLL + k], xs, cols[i * UNROLL + k]) for k in range(UNROLL)]
        for k in range(UNROLL):
            t = i * UNROLL + k
            acc[jnp.where(t < count[0], rows[t], local)] += prods[k]
        return 0

    in_chunks(count[0], tile_copies, buf.shape[0], step)
    copies = [
        pltpu.make_async_copy(acc.at[pl.ds(0, local), rows_of(rank, k)], out, sems.at[k])
        for k, out in enumerate(outs)
    ]
    start(copies)
    wait(copies)


def in_chunks(live, tile_copies, slots, step):
    steps = (live + UNROLL - 1) // UNROLL
    per = slots // CHUNKS // UNROLL
    for i, copy in enumerate(tile_copies):
        copy.wait()
        lax.fori_loop(i * per, jnp.clip(steps, i * per, (i + 1) * per), step, 0)


def forward_first_kernel(
    rank, count, rows, cols, embed, scale, a0, a1, a2, a3, a4, a5, a6, a7, tiles, o0, o1, o2, o3,
    buf, xs, acc, gathered, sems, more, emb, sc,
):
    local = embed.shape[0]
    first = both(embed, scale, emb, sc, sems)
    copies = start_gathered(rank[0], (a0, a1, a2, a3, a4, a5, a6, a7), gathered, more)
    tile_copies = copies_of(tiles, buf, sems, CHUNKS)
    start(tile_copies[:EARLY])

    acc[...] = jnp.zeros_like(acc)
    wait(first)

    def split_own(c, _):
        store_split(xs, c, emb[c] * wide(sc[c]))
        return 0

    lax.fori_loop(0, local, split_own, 0)
    for place, copy in zip(PLACES, copies):
        copy.wait()
        split_piece(rank[0], place, gathered, xs, local)
    start(tile_copies[EARLY:])
    forward_sums(rank[0], count, rows, cols, (o0, o1, o2, o3), buf, xs, acc, tile_copies, sems)


def forward_next_kernel(
    rank, count, rows, cols, scale, p0, p1, p2, p3, arrived, tiles, o0, o1, o2, o3,
    buf, xs, acc, got, sems, more,
):
    local = scale.shape[0]
    copies = copies_of(arrived, got, more, PIECES)
    start(copies)
    tile_copies = copies_of(tiles, buf, sems, CHUNKS)
    start(tile_copies[:EARLY])
    place_quarters(rank[0], (p0, p1, p2, p3), acc)

    def split_own(c, _):
        s = wide(scale[c])
        store_split(xs, c, acc[c] * s * s)
        return 0

    lax.fori_loop(0, local, split_own, 0)
    acc[...] = jnp.zeros_like(acc)
    per = got.shape[0] // PIECES
    for i, copy in enumerate(copies):
        copy.wait()

        def split_arrived(c, _):
            store_split(xs, local + c, got[c])
            return 0

        lax.fori_loop(i * per, (i + 1) * per, split_arrived, 0, unroll=2)
    start(tile_copies[EARLY:])
    forward_sums(rank[0], count, rows, cols, (o0, o1, o2, o3), buf, xs, acc, tile_copies, sems)


def clear(acc, begin):
    def one(c, _):
        acc[c] = jnp.zeros(acc.shape[1:], jnp.float32)
        return 0

    lax.fori_loop(begin, acc.shape[0] - 1, one, 0, unroll=2)


def backward_sums(count, rows, cols, buf, zs, acc, tile_copies):
    readable = acc.shape[0] - 1
    start(tile_copies[EARLY:])

    def step(i, _):
        prods = [product(buf[i * UNROLL + k].T, zs, rows[i * UNROLL + k]) for k in range(UNROLL)]
        for k in range(UNROLL):
            t = i * UNROLL + k
            acc[jnp.where(t < count[0], cols[t], readable)] += prods[k]
        return 0

    in_chunks(count[0], tile_copies, buf.shape[0], step)


def backward_first_kernel(
    count, rows, cols, scale, cot, tiles, out_local, out_remote, buf, zs, acc, sems, more, ct, sc
):
    local, remote = out_local.shape[0], out_remote.shape[0]
    first = both(cot, scale, ct, sc, sems)
    tile_copies = copies_of(tiles, buf, sems, CHUNKS)
    start(tile_copies[:EARLY])

    clear(acc, 0)
    wait(first)

    def prepare(b, _):
        store_split(zs, b, ct[b] / 3.0 * wide(sc[b]))
        return 0

    lax.fori_loop(0, local, prepare, 0)
    backward_sums(count, rows, cols, buf, zs, acc, tile_copies)
    copies = [
        pltpu.make_async_copy(acc.at[pl.ds(local, remote)], out_remote, more.at[0]),
        pltpu.make_async_copy(acc.at[pl.ds(0, local)], out_local, more.at[1]),
    ]
    start(copies)
    wait(copies)


def backward_next_kernel(
    rank, count, rows, cols, scale, cot, q0, q1, q2, q3, tiles, o0, o1, o2, o3, o4, o5, o6, o7,
    buf, zs, acc, sems, more, ct, sc,
):
    first = both(cot, scale, ct, sc, sems)
    tile_copies = copies_of(tiles, buf, sems, CHUNKS)
    start(tile_copies[:EARLY])
    clear(acc, cot.shape[0])
    place_quarters(rank[0], (q0, q1, q2, q3), acc)
    wait(first)

    def prepare(b, _):
        s = wide(sc[b])
        store_split(zs, b, (ct[b] / 3.0 + s * acc[b]) * s)
        acc[b] = jnp.zeros(acc.shape[1:], jnp.float32)
        return 0

    lax.fori_loop(0, cot.shape[0], prepare, 0)
    backward_sums(count, rows, cols, buf, zs, acc, tile_copies)
    half = o0.shape[0]
    copies = []
    for i, out in enumerate((o0, o1, o2, o3, o4, o5, o6, o7)):
        source = acc.at[pl.ds(i % 2 * half, half), rows_of(rank[0], i // 2)]
        copies.append(pltpu.make_async_copy(source, out, more.at[i]))
    start(copies)
    wait(copies)


def own_rows_kernel(targets, local, returned, out):
    out[...] = local[...]

    def one(r, _):
        out[targets[r]] += returned[r]
        return 0

    lax.fori_loop(0, returned.shape[0], one, 0, unroll=2)


def collect_kernel(rank, targets, local, returned, after, o0, o1, o2, o3, acc, got, sems):
    own = pltpu.make_async_copy(local, acc, sems.at[PIECES])
    own.start()
    copies = copies_of(returned, got, sems, PIECES)
    start(copies)
    own.wait()
    per = got.shape[0] // PIECES
    for i, copy in enumerate(copies):
        copy.wait()

        def one(r, _, i=i):
            acc[targets[i * per + r]] += got[i * per + r]
            return 0

        lax.fori_loop(0, per, one, 0, unroll=2)
    take_quarters(rank[0], acc, (o0, o1, o2, o3))


def adam_kernel(
    rank, scale, cot, embed, first, second, q0, q1, q2, q3, new_embed, new_first, new_second
):
    place_quarters(rank[0], (q0, q1, q2, q3), new_first)

    def one(b, _):
        grad = cot[b] / 3.0 + wide(scale[b]) * new_first[b]
        m = 0.9 * first[b] + 0.1 * grad
        v = 0.999 * second[b] + 0.001 * grad * grad
        new_first[b] = m
        new_second[b] = v
        step = m / (1.0 - 0.9**STEP)
        new_embed[b] = embed[b] - 0.01 * step / (jnp.sqrt(v / (1.0 - 0.999**STEP)) + 1e-08)
        return 0

    lax.fori_loop(0, embed.shape[0], one, 0)


def call(kernel, outs, ins, args, us, scratch=(), out_spec=VMEM, mib=60):
    return pl.pallas_call(
        kernel,
        out_shape=outs,
        in_specs=ins,
        out_specs=[out_spec] * len(outs),
        scratch_shapes=scratch,
        compiler_params=pltpu.CompilerParams(vmem_limit_bytes=mib * 2**20),
        cost_estimate=pl.CostEstimate(flops=0, bytes_accessed=int(us * 3.6e6), transcendentals=0),
    )(*args)


def shifted(x, by):
    n = lax.axis_size("grp")
    return lax.ppermute(x, "grp", [(i, (i + by) % n) for i in range(n)])


def helper_sum(parts):
    return parts[0] + shifted(parts[1], 1) + shifted(parts[2], 2) + shifted(parts[3], 3)


def shared(own):
    return (own, shifted(own, 1), shifted(own, 2), shifted(own, 3))


def spread(low, high):
    a1, c2 = shifted(low, 1), shifted(high, 3)
    a2, c1 = shifted(high, 1), shifted(low, 3)
    return (low, high, a1, c2, a2, c1, shifted(a1, 1), shifted(c2, 3))


def combine(parts):
    own_low, own_high, up_low, up_high, far_low, far_high, down_low, down_high = parts
    via_up, via_down = shifted(far_low, 1), shifted(far_high, 3)
    got_high, got_low = shifted(up_high, 1), shifted(down_low, 3)
    last_low, last_high = shifted(up_low + via_up, 1), shifted(down_high + via_down, 3)
    return (own_low, got_low, last_low), (own_high, got_high, last_high)


def after(x, y):
    return lax.optimization_barrier((x, y))[0]


def exchange(x):
    return lax.all_to_all(x, "dom", split_axis=0, concat_axis=0, tiled=True)


def body(
    embed,
    cotangent,
    first_moment,
    second_moment,
    degrees,
    tiles,
    tile_rows,
    tile_cols,
    tile_count,
    send_list,
):
    block = tiles.shape[-1]
    feature = embed.shape[1]
    local = embed.shape[0] // block
    remote = send_list.shape[1] * send_list.shape[2]
    slots = tiles.shape[2]
    rank = lax.axis_index("grp").astype(jnp.int32).reshape(1)
    scale = 1.0 / jnp.sqrt(degrees.astype(jnp.float32))
    scale = jnp.broadcast_to(scale.reshape(local, block, 1), (local, block, 128))
    mats = tiles[0, 0]
    rows, cols, count = tile_rows[0, 0], tile_cols[0, 0], tile_count[0]
    targets = send_list.reshape(remote)
    as_blocks = lambda x: x.reshape(local, block, feature)
    emb, cot = as_blocks(embed), as_blocks(cotangent)
    blocks, sent = f32(local, block, feature), f32(remote, block, feature)
    sent_rows = f32(remote, QUARTER, feature)
    quarters = [f32(local, QUARTER, feature)] * 4
    tile_buf = pltpu.VMEM((slots, block, block), jnp.float32)
    sems = lambda n: pltpu.SemaphoreType.DMA((n,))
    right = lambda n: pltpu.VMEM((n, 2 * block, feature), jnp.bfloat16)
    sums = lambda n: pltpu.VMEM((n, block, feature), jnp.float32)
    some_rows = pltpu.VMEM((local, QUARTER, feature), jnp.float32)
    fwd_scratch = lambda got, n: [
        tile_buf, right(local + remote), sums(local + 1), pltpu.VMEM(got, jnp.float32),
        sems(CHUNKS + 2), sems(n),
    ]
    two = [sums(local), pltpu.VMEM((local, block, 128), jnp.float32)]
    back_scratch = lambda n: [tile_buf, right(local), sums(local + remote + 1), sems(CHUNKS + 2), sems(n), *two]

    (outgoing,) = call(
        first_kernel, [sent_rows], [SMEM] * 2 + [VMEM] * 2, (rank, targets, emb, scale), 2, [some_rows], mib=8
    )
    arrived = exchange(outgoing)
    out_local, out_remote = call(
        backward_first_kernel, [blocks, sent], [SMEM] * 3 + [ANY] * 3,
        (count, rows, cols, scale, cot, mats), 10, back_scratch(2), ANY,
    )
    arrived = after(arrived, out_remote)
    arrived = spread(arrived[: remote // 2], arrived[remote // 2 :])
    parts = call(
        forward_first_kernel, quarters, [SMEM] * 4 + [ANY] * 11,
        (rank, count, rows, cols, emb, scale, *arrived, mats), 10,
        fwd_scratch((4, remote, QUARTER, feature), len(PLACES)) + two, ANY,
    )
    returned = exchange(out_remote)
    collect_scratch = [sums(local), sums(remote), sems(PIECES + 1)]

    def collect(local_sums, returned, after_this):
        return call(
            collect_kernel, quarters, [SMEM] * 2 + [ANY] * 3,
            (rank, targets, local_sums, returned, after_this), 4, collect_scratch, mib=14,
        )

    back = collect(out_local, returned, parts[0])
    parts, back = lax.optimization_barrier((parts, back))
    back = shared(helper_sum(back))
    layer = shared(helper_sum(parts))
    half = (local + remote) // 2
    back = call(
        backward_next_kernel, [f32(half, QUARTER, feature)] * 8, [SMEM] * 4 + [ANY] * 2 + [VMEM] * 4 + [ANY],
        (rank, count, rows, cols, scale, cot, *back, mats), 10, back_scratch(8), ANY,
    )
    first = after(layer[0], back[0])
    low, high = combine(back)
    (outgoing,) = call(
        next_kernel, [sent], [SMEM] * 2 + [VMEM] * 5, (rank, targets, scale, first, *layer[1:]), 3,
        [sums(local), sems(remote)], ANY,
    )
    arrived = exchange(outgoing)
    parts = call(
        forward_next_kernel, quarters, [SMEM] * 4 + [VMEM] * 5 + [ANY] * 2,
        (rank, count, rows, cols, scale, *layer, arrived, mats), 10,
        fwd_scratch((remote, block, feature), PIECES), ANY,
    )
    low, high = low[0] + low[1] + low[2], high[0] + high[1] + high[2]
    own = low[:local]
    returned = exchange(jnp.concatenate([low[local:], high], 0))
    (back,) = call(own_rows_kernel, quarters[:1], [SMEM] + [VMEM] * 2, (targets, own, returned), 2, mib=8)
    parts = [parts[0]] + [shifted(parts[k], k) for k in (1, 2, 3)]
    parts = shared(parts[0] + after(parts[1], back) + parts[2] + parts[3])
    base = after(emb, back)
    (final,) = call(
        final_kernel, [blocks], [SMEM] + [VMEM] * 10, (rank, scale, base, *layer, *parts), 3, mib=10
    )
    back = shared(back)
    new = call(
        adam_kernel, [blocks] * 3, [SMEM] + [VMEM] * 9,
        (rank, scale, cot, emb, as_blocks(first_moment), as_blocks(second_moment), *back), 4, mib=14,
    )
    flat = lambda x: x.reshape(local * block, feature)
    return (flat(final), *(flat(x) for x in new))


def solution(mesh):
    in_specs = (
        P("dom", None),
        P("dom", None),
        P("dom", None),
        P("dom", None),
        P("dom"),
        P("dom", "grp", None, None, None),
        P("dom", "grp", None),
        P("dom", "grp", None),
        P("dom", "grp"),
        P("dom", None, None),
    )
    out_specs = (P("dom", None), P("dom", None), P("dom", None), P("dom", None))
    return jax.shard_map(body, mesh=mesh, in_specs=in_specs, out_specs=out_specs, check_vma=False)
```
